256 devices in a mesh: cfg: 8 (over z_hi, core), row: 8 (over y, z_lo), col: 4 (over x).
Axes of the slice: x: 4, y: 4, z: 8 (z_hi: 4, z_lo: 2; z = z_hi * 2 + z_lo), core: 2. Of those that a mesh axis runs over, the one named last changes fastest.
Arguments:
- sigma_above: float32 [8, 4, 4, 8, 16, 4, 512], P('cfg', None, None, 'row', None, None, 'col'), as said below
- panels: float32 [8, 4, 8, 4, 8, 16, 512], P('cfg', None, None, None, 'row', None, 'col'), may hold values from -0.046875 to 0.046875
- diag_inverse: float32 [8, 4, 4, 8, 16, 512], P('cfg', None, None, 'row', None, 'col'), as said below
- pattern: int32 [8, 4], replicated, may hold values from 0 to 1, as said below
- cfg_weight: float32 [8], P('cfg'), may hold values from 0.2 to 1
Outputs:
- selected: float32 [8, 4, 8, 16, 4, 512], P('cfg', None, 'row', None, None, 'col')
The draws below stay inside these ranges and needn't reach their ends.
Inputs may be any that keep to these rules, and one draw needn't show every extreme that they name: pattern[l, j] is 0 for l <= j and 1 for l = j + 1; for l > j + 1 it is 0 or 1. Each configuration's sigma_above is a symmetric matrix of order 4 * 512. Each diag_inverse[g, j] is a symmetric matrix of order 512.
All inputs are finite; a program needn't handle non-finite values.
Results may differ from the reference program's by a relative error of at most 0.0001.
Values sent between devices are 32-bit elements; how exact they have to be, the bound alone decides.
A program may use at most 64 MiB of HBM per device.

```python
import math
import jax
import jax.numpy as jnp
from jax import lax

B = 512
W = 4
RB = 4
NB = 8
NCFG = 8
GRID_ROWS = 8
GRID_COLS = 4
SUB = 16


def symmetric_draw(noise, matrix_order, lift, spread):
    rows = lax.broadcasted_iota(jnp.int32, (matrix_order, matrix_order), 0)
    cols = lax.broadcasted_iota(jnp.int32, (matrix_order, matrix_order), 1)
    identity = (rows == cols).astype(jnp.float32)
    return (noise + jnp.swapaxes(noise, -1, -2)) * (spread / math.sqrt(matrix_order)) + lift * identity


def draw_sigma_above(key, part):
    key = jax.random.fold_in(key, 1)
    matrix_order = RB * B
    noise_key = jax.random.fold_in(key, 0)
    noise = jax.random.normal(noise_key, (NCFG, matrix_order, matrix_order), jnp.float32)
    sigma = symmetric_draw(noise, matrix_order, 2.0, 0.5)
    return sigma.reshape(NCFG, RB, GRID_COLS, GRID_ROWS, SUB, RB, B)


def draw_diag_inverse(key, part):
    key = jax.random.fold_in(key, 2)
    noise = jax.random.normal(key, (NCFG, W, B, B), jnp.float32)
    inverse = symmetric_draw(noise, B, 1.0, 0.3)
    return inverse.reshape(NCFG, W, GRID_COLS, GRID_ROWS, SUB, B)


def draw_pattern(key, part):
    key = jax.random.fold_in(key, 3)
    coins = (jax.random.randint(key, (NB, W), 0, 5) < 3).astype(jnp.int32)
    rows = lax.broadcasted_iota(jnp.int32, (NB, W), 0)
    cols = lax.broadcasted_iota(jnp.int32, (NB, W), 1)
    chosen = jnp.where(rows == cols + 1, 1, jnp.where(rows > cols + 1, coins, 0))
    return chosen.astype(jnp.int32)


def block_levels(rng, shape, shards, least, top_value):
    def one(dim, parts):
        draws = jax.random.uniform(jax.random.fold_in(jax.random.fold_in(rng, 6), dim), (parts,), jnp.float32, least / len(shards), top_value / len(shards))
        return jnp.repeat(jnp.exp(draws), shape[dim] // parts).reshape((-1,) + (1,) * (len(shape) - dim - 1))

    level = one(*shards[0])
    for cut in shards[1:]:
        level = level * one(*cut)
    return level


def centred(own_key, extent, width, most, cuts=(), kind=jnp.bfloat16):
    array = jax.random.normal(own_key, extent, jnp.float32) * width
    if len(cuts) > 0:
        array = block_levels(own_key, extent, cuts, -0.22, 0.18) * array
    return jnp.clip(array, min=-most, max=most).astype(kind)


def setup_inputs(seed: int = 0) -> dict:
    splits = jax.random.split(jax.random.key(seed), 6)
    sigma_above = draw_sigma_above(jax.random.fold_in(splits[5], 71), 0)
    panels = centred(splits[1], (NCFG, W, NB, GRID_COLS, GRID_ROWS, SUB, B), (4 * NB * B) ** -0.5, 0.046875, ((0, 8), (4, 8), (6, 4)), jnp.float32)
    diag_inverse = draw_diag_inverse(jax.random.fold_in(splits[5], 71), 0)
    pattern = draw_pattern(jax.random.fold_in(splits[5], 71), 0)
    cfg_weight = jnp.clip(0.2 + 0.8 * jax.random.uniform(splits[4], (NCFG,), jnp.float32) ** block_levels(splits[4], (NCFG,), ((0, 8),), -0.2, 0.2), 0.2, 1.0)
    return {"sigma_above": sigma_above, "panels": panels, "diag_inverse": diag_inverse, "pattern": pattern, "cfg_weight": cfg_weight}


def reference(sigma_above, panels, diag_inverse, pattern, cfg_weight):
    matrix_order = NB * B
    highest = lax.Precision.HIGHEST
    pattern_f = pattern.astype(jnp.float32)
    selector = pattern_f + jnp.eye(NB, W, dtype=jnp.float32)
    weighted_sum = jnp.zeros((NB, B, W, B), jnp.float32)
    for config in range(NCFG):
        sigma_state = jnp.zeros((matrix_order, matrix_order), jnp.float32)
        sigma_state = sigma_state.at[W * B:, W * B:].set(sigma_above[config].reshape(RB * B, RB * B))
        for column in reversed(range(W)):
            start = (column + 1) * B
            panel_mat = panels[config, column].reshape(NB, B, B) * pattern_f[:, column][:, None, None]
            panel_mat = panel_mat.reshape(matrix_order, B)[start:]
            row_block = -jnp.dot(panel_mat.T, sigma_state[start:, start:], precision=highest, preferred_element_type=jnp.float32)
            sigma_state = sigma_state.at[column * B:start, start:].set(row_block)
            sigma_state = sigma_state.at[start:, column * B:start].set(row_block.T)
            diagonal = diag_inverse[config, column].reshape(B, B) - jnp.dot(panel_mat.T, row_block.T, precision=highest, preferred_element_type=jnp.float32)
            sigma_state = sigma_state.at[column * B:start, column * B:start].set(diagonal)
        chosen = sigma_state[:, :W * B].reshape(NB, B, W, B) * selector[:, None, :, None]
        weighted_sum = weighted_sum + cfg_weight[config] * chosen
    return weighted_sum.reshape(NB, GRID_COLS, GRID_ROWS, SUB, W, B)
```

```python
import jax
import jax.numpy as jnp
from jax import lax
from jax.experimental import pallas as pl
from jax.experimental.pallas import tpu as pltpu
from jax.sharding import PartitionSpec as P

MESH = pl.DeviceIdType.MESH
F32 = jnp.float32
BF16 = jnp.bfloat16
W = 4
NB = 8
ROWS = 8
COLS = 4
GROUPS = 4
SUB = 16
TR = 64
TC = 128
FULL = 512
WINDOW_BLOCKS = ((3, 2), (3, 1), (2, 1), (3, 0), (2, 0), (1, 0))
WINDOW_PHASES = ((0, 1), (1, 2), (3, 3))


def split(x):
    hi = x.astype(BF16)
    return hi, (x - hi.astype(F32)).astype(BF16)


def dot3(ah, al, bh, bl, dims=(((1,), (0,)), ((), ()))):
    def one(a, b):
        return lax.dot_general(a, b, dims, preferred_element_type=F32)

    return one(ah, bh) + (one(ah, bl) + one(al, bh))


def kernel(
    a_ref, u_ref, d_ref, pat_ref, w_ref, out_ref,
    tr, zx0, zx1, zx2, zx3, zr0, zr1, zr2, zr3, ax, dg,
    ah, al, dh, dl, th, tl, zh0, zh1, zh2, zh3, zl0, zl1, zl2, zl3, bh, bl, qh, ql,
    pw, pa, rw, ra, gw, hb, kb,
    send, recv, send1, recv1,
):
    zx, zr = (zx0, zx1, zx2, zx3), (zr0, zr1, zr2, zr3)
    zh, zl = (zh0, zh1, zh2, zh3), (zl0, zl1, zl2, zl3)
    g, r, c = lax.axis_index("cfg"), lax.axis_index("row"), lax.axis_index("col")
    z_hi, core = lax.div(g, 2), lax.rem(g, 2)
    other = 1 - core
    row_peers = [lax.rem(r + d, ROWS) for d in range(1, ROWS)]
    col_peers = [lax.rem(c + d, COLS) for d in range(1, COLS)]
    z_peers = [lax.rem(z_hi + d, 4) for d in range(1, 4)]
    sibling = {"cfg": 2 * z_hi + other}

    barrier = pltpu.get_barrier_semaphore()
    everyone = [{"row": p} for p in row_peers] + [{"col": p} for p in col_peers]
    everyone += [{"cfg": 2 * p + core} for p in z_peers] + [sibling]
    for peer in everyone:
        pl.semaphore_signal(barrier, inc=1, device_id=peer, device_id_type=MESH)
    pl.semaphore_wait(barrier, len(everyone))

    waits = []

    def put(src, dst, phase, peer):
        pltpu.make_async_remote_copy(
            src_ref=src, dst_ref=dst, send_sem=send.at[phase], recv_sem=recv.at[phase],
            device_id=peer, device_id_type=MESH,
        ).start()

    def take(phase, ref):
        pltpu.make_async_copy(ref, ref, recv.at[phase]).wait()
        waits.append((phase, ref))

    def over_rows(src, dst, phase):
        for p in row_peers:
            put(src, dst, phase, {"row": p})

    def over_cols(src, dst, phase):
        for p in col_peers:
            put(src, dst, phase, {"col": p})

    X, R, T, A, D, F2, F3 = 0, 4, 8, 11, 12, 13, 17

    def panel(k, j):
        return u_ref[j, k] * pat_ref[k, j].astype(F32)

    def send_z(j):
        over_cols(zx[j].at[c], zx[j].at[c], X + j)
        over_rows(zx[j].at[c], zr[j].at[r], R + j)

    def take_x(j):
        take(X + j, zx[j].at[pl.ds(0, COLS - 1)])
        for q in range(COLS):
            hi, lo = split(zx[j][q].reshape(-1, TC))
            zh[j][:, q * TC:(q + 1) * TC] = hi
            zl[j][:, q * TC:(q + 1) * TC] = lo

    def take_t(phase):
        first, count = WINDOW_PHASES[phase]
        take(T + phase, tr.at[pl.ds(0, ROWS - 1), pl.ds(first, count)])
        for s in range(first, first + count):
            for q in range(ROWS):
                hi, lo = split(tr[q, s].reshape(GROUPS, SUB, TC))
                th[s, :, q] = hi
                tl[s, :, q] = lo

    for s, (i, j) in enumerate(WINDOW_BLOCKS):
        tr[r, s] = panel(i, j)
    for k in range(W, NB):
        block = -panel(k, 3)
        zx[3][c, k - 4] = block
        zr[3][r, k - 4] = block

    def send_t(phase):
        first, count = WINDOW_PHASES[phase]
        piece = tr.at[r, pl.ds(first, count)]
        over_rows(piece, piece, T + phase)

    send_t(0)
    over_cols(zx[3].at[c], zx[3].at[c], X + 3)
    send_t(1)
    over_rows(zx[3].at[c], zr[3].at[r], R + 3)
    send_t(2)
    for k in range(1, W):
        dg[c, k - 1] = d_ref[k]
    over_cols(dg.at[c], dg.at[c], D)
    over_cols(a_ref, ax.at[c], A)
    ax[c] = a_ref[...]

    for j in (2, 1, 0):
        take_t(2 - j)
        take_x(j + 1)
        blocks = NB - 1 - j
        acc = [-panel(k, j) for k in range(j + 1, NB)]
        for i in range(j + 1, W):
            s = WINDOW_BLOCKS.index((i, j))
            part = dot3(
                zh[i][...], zl[i][...], th[s].reshape(FULL, TC), tl[s].reshape(FULL, TC)
            ).reshape(NB - 1 - i, TR, TC)
            for k in range(i + 1, NB):
                acc[k - j - 1] -= part[k - i - 1]
        for m in range(blocks):
            zx[j][c, m] = acc[m]
            zr[j][r, m] = acc[m]
        send_z(j)

    take(A, ax.at[pl.ds(0, COLS - 1)])
    for q in range(COLS):
        for m in range(4):
            hi, lo = split(ax[q, :, m, :])
            lanes = slice(m * FULL + q * TC, m * FULL + (q + 1) * TC)
            ah[:, lanes] = hi
            al[:, lanes] = lo
    take(D, dg.at[pl.ds(0, COLS - 1)])
    for q in range(COLS):
        for k in range(3):
            hi, lo = split(dg[q, k])
            dh[k, :, q * TC:(q + 1) * TC] = hi
            dl[k, :, q * TC:(q + 1) * TC] = lo

    weight = w_ref[0]

    def column(j):
        blocks = NB - 1 - j
        take(R + j, zr[j].at[pl.ds(0, ROWS - 1)])
        for q in range(ROWS):
            hi, lo = split(zr[j][q].reshape(blocks, GROUPS, SUB, TC))
            bh[0:blocks, :, q] = hi
            bl[0:blocks, :, q] = lo
        first = blocks - 4
        q_above = weight * dot3(
            ah[...], al[...],
            bh[first:blocks].reshape(4 * FULL, TC), bl[first:blocks].reshape(4 * FULL, TC),
        )
        hi, lo = split(q_above)
        qh[first * TR:blocks * TR, :] = hi
        ql[first * TR:blocks * TR, :] = lo
        q_above = q_above.reshape(4, TR, TC)
        for m in range(4):
            pa[j, m] = q_above[m]
        inside = []
        for m in range(first):
            k = j + 1 + m
            q_in = weight * dot3(
                dh[k - 1], dl[k - 1], bh[m].reshape(FULL, TC), bl[m].reshape(FULL, TC)
            )
            hi, lo = split(q_in)
            qh[m * TR:(m + 1) * TR, :] = hi
            ql[m * TR:(m + 1) * TR, :] = lo
            inside.append(q_in)
        for l in range(j, W):
            start = (l - j) * TR
            part = dot3(
                zh[l][...], zl[l][...],
                qh[start:blocks * TR, :], ql[start:blocks * TR, :],
                (((0,), (0,)), ((), ())),
            ).reshape(GROUPS, ROWS, SUB, TC)
            for q in range(ROWS):
                pw[j, l, q] = part[:, q].reshape(TR, TC)
            pw[j, l, r] += weight * d_ref[j] if l == j else inside[l - j - 1]

    pairs = []

    def to_sibling(slot, src, dst):
        copy = pltpu.make_async_remote_copy(
            src_ref=src, dst_ref=dst, send_sem=send1.at[slot], recv_sem=recv1.at[slot],
            device_id=sibling, device_id_type=MESH,
        )
        copy.start()
        pairs.append(copy)
        return copy

    def finish(lo, count, slot, phase):
        js = pl.ds(lo, count)
        both = [j for j in range(lo, lo + count) if j < 2]
        bs = pl.ds(both[0], len(both))
        copies = [
            to_sibling(slot, pw.at[js, 2 + other], rw.at[js, 1]),
            to_sibling(slot + 1, pw.at[bs, other], rw.at[bs, 0]),
            to_sibling(slot + 2, pa.at[js, other], ra.at[js, 0]),
            to_sibling(slot + 3, pa.at[js, 2 + other], ra.at[js, 1]),
        ]
        copies[0].wait_recv()
        for j in range(lo, lo + count):
            rw[j, 1] += pw[j, 2 + core]
            gw[j, 1, r] = rw[j, 1, r]
        for p in row_peers:
            put(rw.at[js, 1, p], gw.at[js, 1, r], F2 + phase, {"row": p})
        copies[1].wait_recv()
        for j in both:
            rw[j, 0] += pw[j, core]
            gw[j, 0, r] = rw[j, 0, r]
        for p in row_peers:
            put(rw.at[bs, 0, p], gw.at[bs, 0, r], F2 + 2 + phase, {"row": p})
        copies[2].wait_recv()
        copies[3].wait_recv()
        for j in range(lo, lo + count):
            hb[2, j] = pa[j, core] + ra[j, 0]
            hb[3, j] = pa[j, 2 + core] + ra[j, 1]
        take(F2 + phase, gw.at[js, 1, pl.ds(0, ROWS - 1)])
        take(F2 + 2 + phase, gw.at[bs, 0, pl.ds(0, ROWS - 1)])
        for j in range(lo, lo + count):
            hb[1, j] = jnp.sum(gw[j, 1], axis=0)
            hb[0, j] = jnp.sum(gw[j, 0], axis=0) if j in both else jnp.zeros((TR, TC), F32)
        for p in z_peers:
            put(hb.at[p, js], kb.at[z_hi, js], F3 + phase, {"cfg": 2 * p + core})
        kb[z_hi, js] = hb[z_hi, js]
        take(F3 + phase, kb.at[pl.ds(0, 3), js])
        for j in range(lo, lo + count):
            chosen = (pat_ref[g, j] + (g == j).astype(jnp.int32)).astype(F32)
            out_ref[:, j, :] = jnp.sum(kb[:, j], axis=0) * chosen

    pw[3, 2] = jnp.zeros((ROWS, TR, TC), F32)
    pw[1, 0] = jnp.zeros((ROWS, TR, TC), F32)
    column(3)
    column(2)
    column(1)
    finish(1, 3, 0, 0)
    take_x(0)
    column(0)
    finish(0, 1, 4, 1)

    for phase, ref in waits:
        pltpu.make_async_copy(ref, ref, send.at[phase]).wait()
    for copy in pairs:
        copy.wait_send()


def local(sigma_above, panels, diag_inverse, pattern, cfg_weight):
    vmem = pl.BlockSpec(memory_space=pltpu.VMEM)
    smem = pl.BlockSpec(memory_space=pltpu.SMEM)
    tiles = [NB - 1 - j for j in range(W)]
    scratch = [pltpu.VMEM((ROWS, 6, TR, TC), F32)]
    scratch += [pltpu.VMEM((COLS, n, TR, TC), F32) for n in tiles]
    scratch += [pltpu.VMEM((ROWS, n, TR, TC), F32) for n in tiles]
    scratch += [pltpu.VMEM((COLS, 4 * TR, 4, TC), F32), pltpu.VMEM((COLS, 3, TR, TC), F32)]
    scratch += [pltpu.VMEM((4 * TR, 4 * FULL), BF16)] * 2
    scratch += [pltpu.VMEM((3, TR, FULL), BF16)] * 2
    scratch += [pltpu.VMEM((6, GROUPS, ROWS, SUB, TC), BF16)] * 2
    scratch += [pltpu.VMEM((n * TR, FULL), BF16) for n in tiles] * 2
    scratch += [pltpu.VMEM((7, GROUPS, ROWS, SUB, TC), BF16)] * 2
    scratch += [pltpu.VMEM((7 * TR, TC), BF16)] * 2
    scratch += [
        pltpu.VMEM((4, 4, ROWS, TR, TC), F32),
        pltpu.VMEM((4, 4, TR, TC), F32),
        pltpu.VMEM((4, 2, ROWS, TR, TC), F32),
        pltpu.VMEM((4, 2, TR, TC), F32),
        pltpu.VMEM((4, 2, ROWS, TR, TC), F32),
        pltpu.VMEM((4, 4, TR, TC), F32),
        pltpu.VMEM((4, 4, TR, TC), F32),
        pltpu.SemaphoreType.DMA((19,)),
        pltpu.SemaphoreType.DMA((19,)),
        pltpu.SemaphoreType.DMA((8,)),
        pltpu.SemaphoreType.DMA((8,)),
    ]
    out = pl.pallas_call(
        kernel,
        name="selected_inverse",
        out_shape=jax.ShapeDtypeStruct((TR, W, TC), F32),
        in_specs=[vmem, vmem, vmem, smem, smem],
        out_specs=vmem,
        scratch_shapes=scratch,
        compiler_params=pltpu.CompilerParams(
            collective_id=0, has_side_effects=True, vmem_limit_bytes=56 << 20
        ),
    )(
        sigma_above.reshape(4 * TR, 4, TC),
        panels.reshape(W, NB, TR, TC),
        diag_inverse.reshape(W, TR, TC),
        pattern,
        cfg_weight,
    )
    return out.reshape(1, GROUPS, 1, SUB, W, TC)


def solution(mesh):
    return jax.shard_map(
        local,
        mesh=mesh,
        in_specs=(
            P("cfg", None, None, "row", None, None, "col"),
            P("cfg", None, None, None, "row", None, "col"),
            P("cfg", None, None, "row", None, "col"),
            P(),
            P("cfg"),
        ),
        out_specs=P("cfg", None, "row", None, None, "col"),
        check_vma=False,
    )
```

```python
import jax
import jax.numpy as jnp
from jax import lax
from jax.experimental import pallas as pl
from jax.experimental.pallas import tpu as pltpu
from jax.sharding import PartitionSpec as P

MESH = pl.DeviceIdType.MESH
F32 = jnp.float32
BF16 = jnp.bfloat16
W = 4
NB = 8
ROWS = 8
COLS = 4
GROUPS = 4
SUB = 16
TR = 64
TC = 128
FULL = 512
WINDOW_BLOCKS = ((3, 2), (3, 1), (2, 1), (3, 0), (2, 0), (1, 0))
WINDOW_PHASES = ((0, 1), (1, 2), (3, 3))
WINDOW_LATER = {1: (0, 1), 0: (1, 2)}


def split(x):
    hi = x.astype(BF16)
    return hi, (x - hi.astype(F32)).astype(BF16)


def dot3(ah, al, bh, bl, dims=(((1,), (0,)), ((), ()))):
    def one(a, b):
        return lax.dot_general(a, b, dims, preferred_element_type=F32)

    return one(ah, bh) + (one(ah, bl) + one(al, bh))


def kernel(
    a_ref, u_ref, d_ref, pat_ref, w_ref, out_ref,
    tr, zx0, zx1, zx2, zx3, zr, zw, az, ax, dg, qs, qr,
    ah, al, dh, dl, th, tl, zh0, zh1, zh2, zh3, zl0, zl1, zl2, zl3, bh, bl, wh, wl, qh, ql,
    pw, pa, rw, ra, gw, hb, kb,
    send, recv, send1, recv1,
):
    zx = (zx0, zx1, zx2, zx3)
    zh, zl = (zh0, zh1, zh2, zh3), (zl0, zl1, zl2, zl3)
    g, r, c = lax.axis_index("cfg"), lax.axis_index("row"), lax.axis_index("col")
    z_hi, core = lax.div(g, 2), lax.rem(g, 2)
    y, z = lax.div(r, 2), lax.rem(r, 2)
    other = 1 - core
    row_peers = [lax.rem(r + d, ROWS) for d in range(1, ROWS)]
    y_peers = [2 * lax.rem(y + d, 4) + z for d in range(1, 4)]
    z_peer = {"row": 2 * y + 1 - z}
    right, left = lax.rem(c + 1, COLS), lax.rem(c + 3, COLS)
    col_peers = [lax.rem(c + d, COLS) for d in range(1, COLS)]
    z_peers = [lax.rem(z_hi + d, 4) for d in range(1, 4)]
    sibling = {"cfg": 2 * z_hi + other}

    barrier = pltpu.get_barrier_semaphore()
    everyone = [{"row": p} for p in row_peers] + [{"col": p} for p in col_peers]
    everyone += [{"cfg": 2 * p + core} for p in z_peers] + [sibling]
    for peer in everyone:
        pl.semaphore_signal(barrier, inc=1, device_id=peer, device_id_type=MESH)
    pl.semaphore_wait(barrier, len(everyone))

    waits = []

    def put(src, dst, phase, peer):
        pltpu.make_async_remote_copy(
            src_ref=src, dst_ref=dst, send_sem=send.at[phase], recv_sem=recv.at[phase],
            device_id=peer, device_id_type=MESH,
        ).start()

    def take(phase, ref):
        pltpu.make_async_copy(ref, ref, recv.at[phase]).wait()
        waits.append((phase, ref))

    def over_rows(src, dst, phase):
        for p in row_peers:
            put(src, dst, phase, {"row": p})

    def over_cols(src, dst, phase):
        for p in col_peers:
            put(src, dst, phase, {"col": p})

    X, R, T, D, F2, F3, WZ, Q, AZ, AR, AL, RR, RL = 0, 4, 8, 11, 12, 18, 21, 23, 27, 28, 30, 32, 33

    def panel(k, j):
        return u_ref[j, k] * pat_ref[j, k].astype(F32)

    def send_z(j):
        over_cols(zx[j].at[c], zx[j].at[c], X + j)
        above = zx[j].at[c, pl.ds(NB - 5 - j, 4)]
        for p in y_peers:
            put(above, zr.at[j, y], R + j, {"row": p})
        for m in range(4):
            zr[j, y, m] = zx[j][c, NB - 5 - j + m]

    def send_w(j):
        slot, count = WINDOW_LATER[j]
        for m in range(count):
            zw[r, slot + m] = zx[j][c, 1 + m]
        piece = zw.at[r, pl.ds(slot, count)]
        over_rows(piece, piece, WZ + j)

    def take_w(j):
        slot, count = WINDOW_LATER[j]
        take(WZ + j, zw.at[pl.ds(0, ROWS - 1), pl.ds(slot, count)])
        for m in range(slot, slot + count):
            for q in range(ROWS):
                hi, lo = split(zw[q, m].reshape(GROUPS, SUB, TC))
                wh[m, :, q] = hi
                wl[m, :, q] = lo

    def take_x(j):
        take(X + j, zx[j].at[pl.ds(0, COLS - 1)])
        for q in range(COLS):
            hi, lo = split(zx[j][q].reshape(-1, TC))
            zh[j][:, q * TC:(q + 1) * TC] = hi
            zl[j][:, q * TC:(q + 1) * TC] = lo

    def take_t(phase):
        first, count = WINDOW_PHASES[phase]
        take(T + phase, tr.at[pl.ds(0, ROWS - 1), pl.ds(first, count)])
        for s in range(first, first + count):
            for q in range(ROWS):
                hi, lo = split(tr[q, s].reshape(GROUPS, SUB, TC))
                th[s, :, q] = hi
                tl[s, :, q] = lo

    def send_t(phase):
        first, count = WINDOW_PHASES[phase]
        for s in range(first, first + count):
            tr[r, s] = panel(*WINDOW_BLOCKS[s])
        piece = tr.at[r, pl.ds(first, count)]
        over_rows(piece, piece, T + phase)

    for m in range(4):
        zx[3][c, m] = -panel(W + m, 3)
    send_z(3)
    for phase in range(3):
        send_t(phase)

    source = lax.broadcasted_iota(jnp.int32, (2 * TC, 2 * TC), 0)
    target = lax.broadcasted_iota(jnp.int32, (2 * TC, 2 * TC), 1)
    parity = lax.rem(lax.div(source, SUB), 2)
    place = parity * TC + lax.div(source, 2 * SUB) * SUB + lax.rem(source, SUB)
    regroup = (place == target).astype(F32).astype(BF16)
    for pair in range(2):
        both = jnp.concatenate([a_ref[:, 2 * pair, :], a_ref[:, 2 * pair + 1, :]], axis=1)
        hi = both.astype(BF16)
        rest = both - hi.astype(F32)
        mid = rest.astype(BF16)
        low = (rest - mid.astype(F32)).astype(BF16)
        out = (
            jnp.dot(hi, regroup, preferred_element_type=F32)
            + jnp.dot(mid, regroup, preferred_element_type=F32)
            + jnp.dot(low, regroup, preferred_element_type=F32)
        )
        az[0, pair] = out[:, :TC]
        az[1, pair] = out[:, TC:]
    put(az.at[1 - z], ax.at[c, z], AZ, z_peer)
    ax[c, z] = az[z]

    def send_a(part, half):
        piece = ax.at[c, half]
        put(piece, piece, AR + part, {"col": right})
        put(piece, piece, AL + part, {"col": left})

    send_a(0, z)
    for k in range(1, W):
        dg[c, k - 1] = d_ref[k]

    def relay_right():
        take(AR, ax.at[left, z])
        put(ax.at[left, z], ax.at[left, z], RR, {"col": right})

    def relay_left():
        take(AL + 1, ax.at[right, 1 - z])
        put(ax.at[right, 1 - z], ax.at[right, 1 - z], RL, {"col": left})

    def minus_product(acc, i, j):
        s = WINDOW_BLOCKS.index((i, j))
        part = dot3(
            zh[i][...], zl[i][...], th[s].reshape(FULL, TC), tl[s].reshape(FULL, TC)
        ).reshape(NB - 1 - i, TR, TC)
        for k in range(i + 1, NB):
            acc[k - j - 1] -= part[k - i - 1]

    for j in (2, 1, 0):
        take_t(2 - j)
        acc = [-panel(k, j) for k in range(j + 1, NB)]
        for i in range(W - 1, j + 1, -1):
            minus_product(acc, i, j)
        take_x(j + 1)
        minus_product(acc, j + 1, j)
        for m in range(NB - 1 - j):
            zx[j][c, m] = acc[m]
        send_z(j)
        if j < 2:
            send_w(j)
        if j == 2:
            take(AZ, ax.at[c, 1 - z])
            send_a(1, 1 - z)
            relay_right()
        if j == 1:
            over_cols(dg.at[c], dg.at[c], D)
            relay_left()

    take(AR + 1, ax.at[left, 1 - z])
    take(AL, ax.at[right, z])
    take(RR, ax.at[0, 0])
    take(RL, ax.at[0, 1])
    for q in range(COLS):
        for p in range(2):
            for m in range(2):
                hi, lo = split(ax[q, m, p])
                lanes = slice((2 * q + p) * TC, (2 * q + p + 1) * TC)
                ah[m * 4 * TR:(m + 1) * 4 * TR, lanes] = hi
                al[m * 4 * TR:(m + 1) * 4 * TR, lanes] = lo
    take(D, dg.at[pl.ds(0, COLS - 1)])
    for q in range(COLS):
        for k in range(3):
            hi, lo = split(dg[q, k])
            dh[k, :, q * TC:(q + 1) * TC] = hi
            dl[k, :, q * TC:(q + 1) * TC] = lo

    weight = w_ref[0]

    def half_column(j):
        take(R + j, zr.at[j, pl.ds(0, 3)])
        for q in range(4):
            for m in range(4):
                hi, lo = split(zr[j, q, m].reshape(GROUPS, SUB, TC))
                bh[:, m, q] = hi
                bl[:, m, q] = lo
        part = weight * dot3(
            ah[...], al[...], bh[...].reshape(2 * FULL, TC), bl[...].reshape(2 * FULL, TC)
        )
        qs[j, 0] = part[:4 * TR]
        qs[j, 1] = part[4 * TR:]
        put(qs.at[j, 1 - z], qr.at[j], Q + j, z_peer)

    def column(j):
        blocks = NB - 1 - j
        first = blocks - 4
        take(Q + j, qr.at[j])
        q_above = qs[j, z] + qr[j]
        hi, lo = split(q_above)
        qh[first * TR:blocks * TR, :] = hi
        ql[first * TR:blocks * TR, :] = lo
        q_above = q_above.reshape(4, TR, TC)
        for m in range(4):
            pa[j, m] = q_above[m]
        inside = []
        for m in range(first):
            k = j + 1 + m
            if m == 0:
                s = WINDOW_BLOCKS.index((k, j))
                q_in = -weight * dot3(
                    dh[k - 1], dl[k - 1], th[s].reshape(FULL, TC), tl[s].reshape(FULL, TC)
                )
            else:
                s = WINDOW_LATER[j][0] + m - 1
                q_in = weight * dot3(
                    dh[k - 1], dl[k - 1], wh[s].reshape(FULL, TC), wl[s].reshape(FULL, TC)
                )
            hi, lo = split(q_in)
            qh[m * TR:(m + 1) * TR, :] = hi
            ql[m * TR:(m + 1) * TR, :] = lo
            inside.append(q_in)
        for l in range(j, W):
            start = (l - j) * TR
            part = dot3(
                zh[l][...], zl[l][...],
                qh[start:blocks * TR, :], ql[start:blocks * TR, :],
                (((0,), (0,)), ((), ())),
            ).reshape(GROUPS, ROWS, SUB, TC)
            for q in range(ROWS):
                pw[j, l, q] = part[:, q].reshape(TR, TC)
            pw[j, l, r] += weight * d_ref[j] if l == j else inside[l - j - 1]

    pairs = []

    def to_sibling(slot, src, dst):
        copy = pltpu.make_async_remote_copy(
            src_ref=src, dst_ref=dst, send_sem=send1.at[slot], recv_sem=recv1.at[slot],
            device_id=sibling, device_id_type=MESH,
        )
        copy.start()
        pairs.append(copy)
        return copy

    def finish(lo, count, phase):
        js = pl.ds(lo, count)
        columns = range(lo, lo + count)
        both = [j for j in columns if j < 2]
        bs = pl.ds(lo, len(both))
        copies = [
            to_sibling(4 * phase, pw.at[js, 2 + other], rw.at[js, 1]),
            to_sibling(4 * phase + 1, pa.at[js, other], ra.at[js, 0]),
            to_sibling(4 * phase + 2, pa.at[js, 2 + other], ra.at[js, 1]),
        ]
        if both:
            copies.append(to_sibling(4 * phase + 3, pw.at[bs, other], rw.at[bs, 0]))
        yield
        copies[0].wait_recv()
        for j in columns:
            rw[j, 1] += pw[j, 2 + core]
            gw[j, 1, r] = rw[j, 1, r]
        for p in row_peers:
            put(rw.at[js, 1, p], gw.at[js, 1, r], F2 + 2 * phase, {"row": p})
        if both:
            copies[3].wait_recv()
            for j in both:
                rw[j, 0] += pw[j, core]
                gw[j, 0, r] = rw[j, 0, r]
            for p in row_peers:
                put(rw.at[bs, 0, p], gw.at[bs, 0, r], F2 + 2 * phase + 1, {"row": p})
        copies[1].wait_recv()
        copies[2].wait_recv()
        for j in columns:
            hb[2, j] = pa[j, core] + ra[j, 0]
            hb[3, j] = pa[j, 2 + core] + ra[j, 1]
        for p in z_peers:
            @pl.when(p >= 2)
            def _():
                put(hb.at[p, js], kb.at[z_hi, js], F3 + phase, {"cfg": 2 * p + core})
        yield
        take(F2 + 2 * phase, gw.at[js, 1, pl.ds(0, ROWS - 1)])
        if both:
            take(F2 + 2 * phase + 1, gw.at[bs, 0, pl.ds(0, ROWS - 1)])
        for j in columns:
            hb[1, j] = jnp.sum(gw[j, 1], axis=0)
            hb[0, j] = jnp.sum(gw[j, 0], axis=0) if j in both else jnp.zeros((TR, TC), F32)
        for p in z_peers:
            @pl.when(p < 2)
            def _():
                put(hb.at[p, js], kb.at[z_hi, js], F3 + phase, {"cfg": 2 * p + core})
        kb[z_hi, js] = hb[z_hi, js]
        yield
        take(F3 + phase, kb.at[pl.ds(0, 3), js])
        for j in columns:
            chosen = (pat_ref[j, g] + (g == j).astype(jnp.int32)).astype(F32)
            out_ref[:, j, :] = jnp.sum(kb[:, j], axis=0) * chosen
        yield

    pw[3, 2] = jnp.zeros((ROWS, TR, TC), F32)
    pw[1, 0] = jnp.zeros((ROWS, TR, TC), F32)
    half_column(3)
    half_column(2)
    half_column(1)
    column(3)
    column(2)
    first = finish(2, 2, 0)
    next(first)
    take_w(1)
    column(1)
    second = finish(1, 1, 1)
    next(second)
    next(first)
    half_column(0)
    next(second)
    take_w(0)
    take_x(0)
    column(0)
    third = finish(0, 1, 2)
    next(third)
    next(first)
    next(second)
    next(third)
    next(third)
    next(first)
    next(second)
    next(third)

    for phase, ref in waits:
        pltpu.make_async_copy(ref, ref, send.at[phase]).wait()
    for copy in pairs:
        copy.wait_send()


def local(sigma_above, panels, diag_inverse, pattern, cfg_weight):
    vmem = pl.BlockSpec(memory_space=pltpu.VMEM)
    smem = pl.BlockSpec(memory_space=pltpu.SMEM)
    tiles = [NB - 1 - j for j in range(W)]
    scratch = [pltpu.VMEM((ROWS, 6, TR, TC), F32)]
    scratch += [pltpu.VMEM((COLS, n, TR, TC), F32) for n in tiles]
    scratch += [pltpu.VMEM((W, 4, 4, TR, TC), F32), pltpu.VMEM((ROWS, 3, TR, TC), F32)]
    scratch += [pltpu.VMEM((2, 2, 4 * TR, TC), F32), pltpu.VMEM((COLS, 2, 2, 4 * TR, TC), F32)]
    scratch += [pltpu.VMEM((COLS, 3, TR, TC), F32)]
    scratch += [pltpu.VMEM((W, 2, 4 * TR, TC), F32), pltpu.VMEM((W, 4 * TR, TC), F32)]
    scratch += [pltpu.VMEM((8 * TR, 2 * FULL), BF16)] * 2
    scratch += [pltpu.VMEM((3, TR, FULL), BF16)] * 2
    scratch += [pltpu.VMEM((6, GROUPS, ROWS, SUB, TC), BF16)] * 2
    scratch += [pltpu.VMEM((n * TR, FULL), BF16) for n in tiles] * 2
    scratch += [pltpu.VMEM((GROUPS, 4, 4, SUB, TC), BF16)] * 2
    scratch += [pltpu.VMEM((3, GROUPS, ROWS, SUB, TC), BF16)] * 2
    scratch += [pltpu.VMEM((7 * TR, TC), BF16)] * 2
    scratch += [
        pltpu.VMEM((4, 4, ROWS, TR, TC), F32),
        pltpu.VMEM((4, 4, TR, TC), F32),
        pltpu.VMEM((4, 2, ROWS, TR, TC), F32),
        pltpu.VMEM((4, 2, TR, TC), F32),
        pltpu.VMEM((4, 2, ROWS, TR, TC), F32),
        pltpu.VMEM((4, 4, TR, TC), F32),
        pltpu.VMEM((4, 4, TR, TC), F32),
        pltpu.SemaphoreType.DMA((34,)),
        pltpu.SemaphoreType.DMA((34,)),
        pltpu.SemaphoreType.DMA((12,)),
        pltpu.SemaphoreType.DMA((12,)),
    ]
    out = pl.pallas_call(
        kernel,
        name="selected_inverse",
        out_shape=jax.ShapeDtypeStruct((TR, W, TC), F32),
        in_specs=[vmem, vmem, vmem, smem, smem],
        out_specs=vmem,
        scratch_shapes=scratch,
        compiler_params=pltpu.CompilerParams(
            collective_id=0, has_side_effects=True, vmem_limit_bytes=56 << 20
        ),
    )(
        sigma_above.reshape(4 * TR, 4, TC),
        panels.reshape(W, NB, TR, TC),
        diag_inverse.reshape(W, TR, TC),
        pattern.T,
        cfg_weight,
    )
    return out.reshape(1, GROUPS, 1, SUB, W, TC)


def solution(mesh):
    return jax.shard_map(
        local,
        mesh=mesh,
        in_specs=(
            P("cfg", None, None, "row", None, None, "col"),
            P("cfg", None, None, None, "row", None, "col"),
            P("cfg", None, None, "row", None, "col"),
            P(),
            P("cfg"),
        ),
        out_specs=P("cfg", None, "row", None, None, "col"),
        check_vma=False,
    )
```

```python
import jax
import jax.numpy as jnp
from jax import lax
from jax.experimental import pallas as pl
from jax.experimental.pallas import tpu as pltpu
from jax.sharding import PartitionSpec as P

MESH = pl.DeviceIdType.MESH
F32 = jnp.float32
BF16 = jnp.bfloat16
W = 4
NB = 8
ROWS = 8
COLS = 4
GROUPS = 4
SUB = 16
TR = 64
TC = 128
FULL = 512
WINDOW_BLOCKS = ((3, 2), (3, 1), (2, 1), (3, 0), (2, 0), (1, 0))
WINDOW_PHASES = ((0, 1), (1, 2), (3, 3))
WINDOW_LATER = {1: (0, 1), 0: (1, 2)}


def split(x):
    hi = x.astype(BF16)
    return hi, (x - hi.astype(F32)).astype(BF16)


def dot3(ah, al, bh, bl, dims=(((1,), (0,)), ((), ()))):
    def one(a, b):
        return lax.dot_general(a, b, dims, preferred_element_type=F32)

    return one(ah, bh) + (one(ah, bl) + one(al, bh))


def kernel(
    a_ref, u_ref, d_ref, pat_ref, w_ref, out_ref,
    tr, zx0, zx1, zx2, zx3, zr, zw, az, ax, dg, qs, qr,
    ah, al, dh, dl, th, tl, zh0, zh1, zh2, zh3, zl0, zl1, zl2, zl3, bh, bl, wh, wl, qh, ql,
    pw, pa, rw, ra, gw, hb, kb,
    send, recv, send1, recv1,
):
    zx = (zx0, zx1, zx2, zx3)
    zh, zl = (zh0, zh1, zh2, zh3), (zl0, zl1, zl2, zl3)
    g, r, c = lax.axis_index("cfg"), lax.axis_index("row"), lax.axis_index("col")
    z_hi, core = lax.div(g, 2), lax.rem(g, 2)
    y, z = lax.div(r, 2), lax.rem(r, 2)
    other = 1 - core
    row_peers = [lax.rem(r + d, ROWS) for d in range(1, ROWS)]
    y_peers = [2 * lax.rem(y + d, 4) + z for d in range(1, 4)]
    z_peer = {"row": 2 * y + 1 - z}
    col_peers = [lax.rem(c + d, COLS) for d in range(1, COLS)]
    z_peers = [lax.rem(z_hi + d, 4) for d in range(1, 4)]
    sibling = {"cfg": 2 * z_hi + other}

    barrier = pltpu.get_barrier_semaphore()
    everyone = [{"row": p} for p in row_peers] + [{"col": p} for p in col_peers]
    everyone += [{"cfg": 2 * p + core} for p in z_peers] + [sibling]
    for peer in everyone:
        pl.semaphore_signal(barrier, inc=1, device_id=peer, device_id_type=MESH)
    pl.semaphore_wait(barrier, len(everyone))

    waits = []
    later_waits = []

    def when(condition, action):
        if condition is None:
            action()
        else:
            pl.when(condition)(action)

    def put(src, dst, phase, peer):
        pltpu.make_async_remote_copy(
            src_ref=src, dst_ref=dst, send_sem=send.at[phase], recv_sem=recv.at[phase],
            device_id=peer, device_id_type=MESH,
        ).start()

    def take(phase, ref):
        pltpu.make_async_copy(ref, ref, recv.at[phase]).wait()
        waits.append((phase, ref))

    def over_rows(src, dst, phase):
        for p in row_peers:
            put(src, dst, phase, {"row": p})

    def over_cols(src, dst, phase):
        for p in col_peers:
            put(src, dst, phase, {"col": p})

    X, R, T, D, F2, F3, WZ, Q, AZ, A = 0, 4, 8, 11, 12, 20, 24, 26, 30, 31

    def panel(k, j):
        return u_ref[j, k] * pat_ref[j, k].astype(F32)

    def send_x(j):
        over_cols(zx[j].at[c], zx[j].at[c], X + j)

    def send_y(j):
        for m in range(4):
            zr[j, y, m] = zx[j][c, NB - 5 - j + m]
        for p in y_peers:
            put(zr.at[j, y], zr.at[j, y], R + j, {"row": p})

    def send_w(j):
        slot, count = WINDOW_LATER[j]
        for m in range(count):
            zw[r, slot + m] = zx[j][c, 1 + m]
        piece = zw.at[r, pl.ds(slot, count)]
        over_rows(piece, piece, WZ + j)

    def take_w(j):
        slot, count = WINDOW_LATER[j]
        take(WZ + j, zw.at[pl.ds(0, ROWS - 1), pl.ds(slot, count)])
        for m in range(slot, slot + count):
            for q in range(ROWS):
                hi, lo = split(zw[q, m].reshape(GROUPS, SUB, TC))
                wh[m, :, q] = hi
                wl[m, :, q] = lo

    def take_x(j):
        take(X + j, zx[j].at[pl.ds(0, COLS - 1)])
        for q in range(COLS):
            hi, lo = split(zx[j][q].reshape(-1, TC))
            zh[j][:, q * TC:(q + 1) * TC] = hi
            zl[j][:, q * TC:(q + 1) * TC] = lo

    def take_t(phase):
        first, count = WINDOW_PHASES[phase]
        take(T + phase, tr.at[pl.ds(0, ROWS - 1), pl.ds(first, count)])
        for s in range(first, first + count):
            for q in range(ROWS):
                hi, lo = split(tr[q, s].reshape(GROUPS, SUB, TC))
                th[s, :, q] = hi
                tl[s, :, q] = lo

    def send_t(phase):
        first, count = WINDOW_PHASES[phase]
        for s in range(first, first + count):
            tr[r, s] = panel(*WINDOW_BLOCKS[s])
        piece = tr.at[r, pl.ds(first, count)]
        over_rows(piece, piece, T + phase)

    send_t(0)
    for m in range(4):
        zx[3][c, m] = -panel(W + m, 3)
    send_x(3)
    send_t(1)
    send_t(2)

    source = lax.broadcasted_iota(jnp.int32, (2 * TC, 2 * TC), 0)
    target = lax.broadcasted_iota(jnp.int32, (2 * TC, 2 * TC), 1)
    parity = lax.rem(lax.div(source, SUB), 2)
    place = parity * TC + lax.div(source, 2 * SUB) * SUB + lax.rem(source, SUB)
    regroup = (place == target).astype(F32).astype(BF16)
    for pair in range(2):
        both = jnp.concatenate([a_ref[:, 2 * pair, :], a_ref[:, 2 * pair + 1, :]], axis=1)
        hi = both.astype(BF16)
        rest = both - hi.astype(F32)
        mid = rest.astype(BF16)
        low = (rest - mid.astype(F32)).astype(BF16)
        out = (
            jnp.dot(hi, regroup, preferred_element_type=F32)
            + jnp.dot(mid, regroup, preferred_element_type=F32)
            + jnp.dot(low, regroup, preferred_element_type=F32)
        )
        az[0, pair] = out[:, :TC]
        az[1, pair] = out[:, TC:]
    put(az.at[1 - z], ax.at[c, z], AZ, z_peer)
    ax[c, z] = az[z]

    for k in range(1, W):
        dg[c, k - 1] = d_ref[k]

    parts = ((z, 0), (z, 1), (1 - z, 0), (1 - z, 1))

    def send_a(part):
        piece = ax.at[(c, *parts[part])]
        over_cols(piece, piece, A + part)

    def take_a(part):
        half, pair = parts[part]
        take(A + part, ax.at[pl.ds(0, COLS - 1), half, pair])
        for q in range(COLS):
            hi, lo = split(ax[q, half, pair])
            lanes = slice((2 * q + pair) * TC, (2 * q + pair + 1) * TC)
            ah[half, :, lanes] = hi
            al[half, :, lanes] = lo

    def take_d():
        take(D, dg.at[pl.ds(0, COLS - 1)])
        for q in range(COLS):
            for k in range(3):
                hi, lo = split(dg[q, k])
                dh[k, :, q * TC:(q + 1) * TC] = hi
                dl[k, :, q * TC:(q + 1) * TC] = lo

    def minus_product(acc, i, j):
        s = WINDOW_BLOCKS.index((i, j))
        part = dot3(
            zh[i][...], zl[i][...], th[s].reshape(FULL, TC), tl[s].reshape(FULL, TC)
        ).reshape(NB - 1 - i, TR, TC)
        for k in range(i + 1, NB):
            acc[k - j - 1] -= part[k - i - 1]

    send_a(0)
    send_a(1)
    send_y(3)

    weight = w_ref[0]

    pairs = []

    def to_sibling(slot, src, dst):
        copy = pltpu.make_async_remote_copy(
            src_ref=src, dst_ref=dst, send_sem=send1.at[slot], recv_sem=recv1.at[slot],
            device_id=sibling, device_id_type=MESH,
        )
        copy.start()
        pairs.append(copy)
        return copy

    above = {}

    def half_column(j):
        take(R + j, zr.at[j, pl.ds(0, 3)])
        for q in range(4):
            for m in range(4):
                hi, lo = split(zr[j, q, m].reshape(GROUPS, SUB, TC))
                bh[:, m, q] = hi
                bl[:, m, q] = lo
        part = weight * dot3(
            ah[...].reshape(8 * TR, 2 * FULL), al[...].reshape(8 * TR, 2 * FULL), bh[...].reshape(2 * FULL, TC), bl[...].reshape(2 * FULL, TC)
        )
        qs[j, 0] = part[:4 * TR]
        qs[j, 1] = part[4 * TR:]
        put(qs.at[j, 1 - z], qr.at[j], Q + j, z_peer)

    def column(j):
        blocks = NB - 1 - j
        first = blocks - 4
        take(Q + j, qr.at[j])
        q_above = qs[j, z] + qr[j]
        hi, lo = split(q_above)
        qh[first * TR:blocks * TR, :] = hi
        ql[first * TR:blocks * TR, :] = lo
        q_above = q_above.reshape(4, TR, TC)
        for m in range(4):
            pa[j, m] = q_above[m]
        above[j] = [
            to_sibling(4 * j + t, pa.at[j, 2 * t + other], ra.at[j, t]) for t in range(2)
        ]
        inside = []
        for m in range(first):
            k = j + 1 + m
            if m == 0:
                s = WINDOW_BLOCKS.index((k, j))
                q_in = -weight * dot3(
                    dh[k - 1], dl[k - 1], th[s].reshape(FULL, TC), tl[s].reshape(FULL, TC)
                )
            else:
                s = WINDOW_LATER[j][0] + m - 1
                q_in = weight * dot3(
                    dh[k - 1], dl[k - 1], wh[s].reshape(FULL, TC), wl[s].reshape(FULL, TC)
                )
            hi, lo = split(q_in)
            qh[m * TR:(m + 1) * TR, :] = hi
            ql[m * TR:(m + 1) * TR, :] = lo
            inside.append(q_in)
        for l in range(j, W):
            start = (l - j) * TR
            part = dot3(
                zh[l][...], zl[l][...],
                qh[start:blocks * TR, :], ql[start:blocks * TR, :],
                (((0,), (0,)), ((), ())),
            ).reshape(GROUPS, ROWS, SUB, TC)
            for q in range(ROWS):
                pw[j, l, q] = part[:, q].reshape(TR, TC)
            pw[j, l, r] += weight * d_ref[j] if l == j else inside[l - j - 1]

    def finish(j):
        slots = [1, 0] if j < 2 else [1]
        used = {t: None if 2 * t >= j else core == 1 for t in slots}
        unused = {t: None if 2 * t >= j else core == 0 for t in slots}
        copies = {}
        for t in slots:
            copies[t] = pltpu.make_async_remote_copy(
                src_ref=pw.at[j, 2 * t + other], dst_ref=rw.at[j, t],
                send_sem=send1.at[4 * j + 2 + t], recv_sem=recv1.at[4 * j + 2 + t],
                device_id=sibling, device_id_type=MESH,
            )
            when(unused[t], copies[t].start)
            later_waits.append((unused[t], copies[t].wait_send))
        yield
        for t in slots:
            def add(t=t):
                copies[t].wait_recv()
                rw[j, t] += pw[j, 2 * t + core]
                gw[j, t, r] = rw[j, t, r]
                for p in row_peers:
                    put(rw.at[j, t, p], gw.at[j, t, r], F2 + 2 * j + t, {"row": p})

            when(used[t], add)
        for t, copy in enumerate(above[j]):
            copy.wait_recv()
            hb[2 + t, j] = pa[j, 2 * t + core] + ra[j, t]
        send_out(j, 2)
        send_out(j, 3)
        yield
        for t in slots:
            def total(t=t):
                piece = gw.at[j, t, pl.ds(0, ROWS - 1)]
                pltpu.make_async_copy(piece, piece, recv.at[F2 + 2 * j + t]).wait()
                hb[t, j] = jnp.sum(gw[j, t], axis=0)

            def sent(t=t):
                piece = gw.at[j, t, pl.ds(0, ROWS - 1)]
                pltpu.make_async_copy(piece, piece, send.at[F2 + 2 * j + t]).wait()

            when(used[t], total)
            later_waits.append((used[t], sent))
            send_out(j, t)
        kb[z_hi, j] = hb[z_hi, j]
        yield
        l = 2 * z_hi + core

        @pl.when(l >= j)
        def _():
            piece = kb.at[pl.ds(0, 3), j]
            pltpu.make_async_copy(piece, piece, recv.at[F3 + j]).wait()
            chosen = (pat_ref[j, g] + (g == j).astype(jnp.int32)).astype(F32)
            out_ref[:, j, :] = jnp.sum(kb[:, j], axis=0) * chosen

        if j > 0:
            @pl.when(l < j)
            def _():
                out_ref[:, j, :] = jnp.zeros((TR, TC), F32)
        yield

    def send_out(j, t):
        condition = z_hi != t
        if 2 * t < j:
            condition = jnp.logical_and(condition, core == 1)

        def copy():
            return pltpu.make_async_remote_copy(
                src_ref=hb.at[t, j], dst_ref=kb.at[z_hi, j], send_sem=send.at[F3 + j],
                recv_sem=recv.at[F3 + j], device_id={"cfg": 2 * t + core}, device_id_type=MESH,
            )

        when(condition, lambda: copy().start())
        later_waits.append((condition, lambda: copy().wait_send()))

    hb[0:2] = jnp.zeros((2, 4, TR, TC), F32)
    for j in (2, 1, 0):
        take_t(2 - j)
        acc = [-panel(k, j) for k in range(j + 1, NB)]
        for i in range(W - 1, j + 1, -1):
            minus_product(acc, i, j)
        if j == 1:
            take_a(0)
            take_a(1)
        if j == 0:
            take_a(2)
            take_a(3)
            half_column(3)
            half_column(2)
        take_x(j + 1)
        minus_product(acc, j + 1, j)
        for m in range(NB - 1 - j):
            zx[j][c, m] = acc[m]
        if j > 0:
            send_x(j)
        send_y(j)
        if j < 2:
            send_w(j)
        if j == 2:
            take(AZ, ax.at[c, 1 - z])
            send_a(2)
            send_a(3)
        if j == 1:
            over_cols(dg.at[c], dg.at[c], D)
        if j == 0:
            send_x(0)

    column(3)
    steps = {3: finish(3)}
    next(steps[3])
    take_d()
    column(2)
    steps[2] = finish(2)
    next(steps[2])
    next(steps[3])
    half_column(1)
    take_w(1)
    next(steps[2])
    column(1)
    steps[1] = finish(1)
    next(steps[1])
    next(steps[3])
    next(steps[1])
    half_column(0)
    next(steps[2])
    take_w(0)
    take_x(0)
    column(0)
    steps[0] = finish(0)
    next(steps[0])
    next(steps[1])
    next(steps[0])
    for j in (3, 2, 1):
        next(steps[j])
    next(steps[0])
    next(steps[0])

    for phase, ref in waits:
        pltpu.make_async_copy(ref, ref, send.at[phase]).wait()
    for copy in pairs:
        copy.wait_send()
    for condition, action in later_waits:
        when(condition, action)


def local(sigma_above, panels, diag_inverse, pattern, cfg_weight):
    vmem = pl.BlockSpec(memory_space=pltpu.VMEM)
    smem = pl.BlockSpec(memory_space=pltpu.SMEM)
    tiles = [NB - 1 - j for j in range(W)]
    scratch = [pltpu.VMEM((ROWS, 6, TR, TC), F32)]
    scratch += [pltpu.VMEM((COLS, n, TR, TC), F32) for n in tiles]
    scratch += [pltpu.VMEM((W, 4, 4, TR, TC), F32), pltpu.VMEM((ROWS, 3, TR, TC), F32)]
    scratch += [pltpu.VMEM((2, 2, 4 * TR, TC), F32), pltpu.VMEM((COLS, 2, 2, 4 * TR, TC), F32)]
    scratch += [pltpu.VMEM((COLS, 3, TR, TC), F32)]
    scratch += [pltpu.VMEM((W, 2, 4 * TR, TC), F32), pltpu.VMEM((W, 4 * TR, TC), F32)]
    scratch += [pltpu.VMEM((2, 4 * TR, 2 * FULL), BF16)] * 2
    scratch += [pltpu.VMEM((3, TR, FULL), BF16)] * 2
    scratch += [pltpu.VMEM((6, GROUPS, ROWS, SUB, TC), BF16)] * 2
    scratch += [pltpu.VMEM((n * TR, FULL), BF16) for n in tiles] * 2
    scratch += [pltpu.VMEM((GROUPS, 4, 4, SUB, TC), BF16)] * 2
    scratch += [pltpu.VMEM((3, GROUPS, ROWS, SUB, TC), BF16)] * 2
    scratch += [pltpu.VMEM((7 * TR, TC), BF16)] * 2
    scratch += [
        pltpu.VMEM((4, 4, ROWS, TR, TC), F32),
        pltpu.VMEM((4, 4, TR, TC), F32),
        pltpu.VMEM((4, 2, ROWS, TR, TC), F32),
        pltpu.VMEM((4, 2, TR, TC), F32),
        pltpu.VMEM((4, 2, ROWS, TR, TC), F32),
        pltpu.VMEM((4, 4, TR, TC), F32),
        pltpu.VMEM((4, 4, TR, TC), F32),
        pltpu.SemaphoreType.DMA((35,)),
        pltpu.SemaphoreType.DMA((35,)),
        pltpu.SemaphoreType.DMA((16,)),
        pltpu.SemaphoreType.DMA((16,)),
    ]
    out = pl.pallas_call(
        kernel,
        name="selected_inverse",
        out_shape=jax.ShapeDtypeStruct((TR, W, TC), F32),
        in_specs=[vmem, vmem, vmem, smem, smem],
        out_specs=vmem,
        scratch_shapes=scratch,
        compiler_params=pltpu.CompilerParams(
            collective_id=0, has_side_effects=True, vmem_limit_bytes=56 << 20
        ),
    )(
        sigma_above.reshape(4 * TR, 4, TC),
        panels.reshape(W, NB, TR, TC),
        diag_inverse.reshape(W, TR, TC),
        pattern.T,
        cfg_weight,
    )
    return out.reshape(1, GROUPS, 1, SUB, W, TC)


def solution(mesh):
    return jax.shard_map(
        local,
        mesh=mesh,
        in_specs=(
            P("cfg", None, None, "row", None, None, "col"),
            P("cfg", None, None, None, "row", None, "col"),
            P("cfg", None, None, "row", None, "col"),
            P(),
            P("cfg"),
        ),
        out_specs=P("cfg", None, "row", None, None, "col"),
        check_vma=False,
    )
```

```python
import jax
import jax.numpy as jnp
from jax import lax
from jax.experimental import pallas as pl
from jax.experimental.pallas import tpu as pltpu
from jax.sharding import PartitionSpec as P

MESH = pl.DeviceIdType.MESH
F32 = jnp.float32
BF16 = jnp.bfloat16
W = 4
NB = 8
ROWS = 8
COLS = 4
GROUPS = 4
SUB = 16
TR = 64
TC = 128
FULL = 512
WINDOW_BLOCKS = ((3, 2), (3, 1), (2, 1), (3, 0), (2, 0), (1, 0))
WINDOW_PHASES = ((0, 1), (1, 2), (3, 3))
WINDOW_LATER = {1: (0, 1), 0: (1, 2)}


def split(x):
    hi = x.astype(BF16)
    return hi, (x - hi.astype(F32)).astype(BF16)


def dot3(ah, al, bh, bl, dims=(((1,), (0,)), ((), ()))):
    def one(a, b):
        return lax.dot_general(a, b, dims, preferred_element_type=F32)

    return one(ah, bh) + (one(ah, bl) + one(al, bh))


def kernel(
    a_ref, u_ref, d_ref, pat_ref, w_hbm, out_ref,
    tr, zx0, zx1, zx2, zx3, zr, zw, az, ax, dg, qs, qr,
    ah, al, dh, dl, th, tl, zh0, zh1, zh2, zh3, zl0, zl1, zl2, zl3, bh, bl, wh, wl, qh, ql,
    pw, pa, rw, ra, gw, hb, kb,
    send, recv, send1, recv1, w_ref, w_sem,
):
    zx = (zx0, zx1, zx2, zx3)
    zh, zl = (zh0, zh1, zh2, zh3), (zl0, zl1, zl2, zl3)
    g, r, c = lax.axis_index("cfg"), lax.axis_index("row"), lax.axis_index("col")
    z_hi, core = lax.div(g, 2), lax.rem(g, 2)
    y, z = lax.div(r, 2), lax.rem(r, 2)
    other = 1 - core
    row_peers = [lax.rem(r + d, ROWS) for d in range(1, ROWS)]
    y_peers = [2 * lax.rem(y + d, 4) + z for d in range(1, 4)]
    z_peer = {"row": 2 * y + 1 - z}
    col_peers = [lax.rem(c + d, COLS) for d in range(1, COLS)]
    z_peers = [lax.rem(z_hi + d, 4) for d in range(1, 4)]
    sibling = {"cfg": 2 * z_hi + other}

    weight_copy = pltpu.make_async_copy(w_hbm, w_ref, w_sem)
    weight_copy.start()
    barrier = pltpu.get_barrier_semaphore()
    everyone = [{"row": p} for p in row_peers] + [{"col": p} for p in col_peers]
    everyone += [{"cfg": 2 * p + core} for p in z_peers] + [sibling]
    for peer in everyone:
        pl.semaphore_signal(barrier, inc=1, device_id=peer, device_id_type=MESH)
    pl.semaphore_wait(barrier, len(everyone))

    waits = []
    later_waits = []

    def when(condition, action):
        if condition is None:
            action()
        else:
            pl.when(condition)(action)

    def put(src, dst, phase, peer):
        pltpu.make_async_remote_copy(
            src_ref=src, dst_ref=dst, send_sem=send.at[phase], recv_sem=recv.at[phase],
            device_id=peer, device_id_type=MESH,
        ).start()

    def take(phase, ref):
        pltpu.make_async_copy(ref, ref, recv.at[phase]).wait()
        waits.append((phase, ref))

    def over_rows(src, dst, phase):
        for p in row_peers:
            put(src, dst, phase, {"row": p})

    def over_cols(src, dst, phase):
        for p in col_peers:
            put(src, dst, phase, {"col": p})

    X, R, T, D, F2, F3, WZ, Q, AZ, A = 0, 4, 8, 11, 12, 20, 24, 26, 30, 31

    def panel(k, j):
        return u_ref[j, k] * pat_ref[j, k].astype(F32)

    def send_x(j):
        over_cols(zx[j].at[c], zx[j].at[c], X + j)

    def send_y(j):
        for m in range(4):
            zr[j, y, m] = zx[j][c, NB - 5 - j + m]
        for p in y_peers:
            put(zr.at[j, y], zr.at[j, y], R + j, {"row": p})

    def send_w(j):
        slot, count = WINDOW_LATER[j]
        for m in range(count):
            zw[r, slot + m] = zx[j][c, 1 + m]
        piece = zw.at[r, pl.ds(slot, count)]
        over_rows(piece, piece, WZ + j)

    def take_w(j):
        slot, count = WINDOW_LATER[j]
        take(WZ + j, zw.at[pl.ds(0, ROWS - 1), pl.ds(slot, count)])
        for m in range(slot, slot + count):
            for q in range(ROWS):
                hi, lo = split(zw[q, m].reshape(GROUPS, SUB, TC))
                wh[m, :, q] = hi
                wl[m, :, q] = lo

    def take_x(j):
        take(X + j, zx[j].at[pl.ds(0, COLS - 1)])
        for q in range(COLS):
            hi, lo = split(zx[j][q].reshape(-1, TC))
            zh[j][:, q * TC:(q + 1) * TC] = hi
            zl[j][:, q * TC:(q + 1) * TC] = lo

    def take_t(phase):
        first, count = WINDOW_PHASES[phase]
        take(T + phase, tr.at[pl.ds(0, ROWS - 1), pl.ds(first, count)])
        for s in range(first, first + count):
            for q in range(ROWS):
                hi, lo = split(tr[q, s].reshape(GROUPS, SUB, TC))
                th[s, :, q] = hi
                tl[s, :, q] = lo

    def send_t(phase):
        first, count = WINDOW_PHASES[phase]
        for s in range(first, first + count):
            tr[r, s] = panel(*WINDOW_BLOCKS[s])
        piece = tr.at[r, pl.ds(first, count)]
        over_rows(piece, piece, T + phase)

    send_t(0)
    for m in range(4):
        zx[3][c, m] = -panel(W + m, 3)
    send_x(3)
    send_t(1)
    send_t(2)

    source = lax.broadcasted_iota(jnp.int32, (2 * TC, 2 * TC), 0)
    target = lax.broadcasted_iota(jnp.int32, (2 * TC, 2 * TC), 1)
    parity = lax.rem(lax.div(source, SUB), 2)
    place = parity * TC + lax.div(source, 2 * SUB) * SUB + lax.rem(source, SUB)
    regroup = (place == target).astype(F32).astype(BF16)
    for pair in range(2):
        both = jnp.concatenate([a_ref[:, 2 * pair, :], a_ref[:, 2 * pair + 1, :]], axis=1)
        hi = both.astype(BF16)
        rest = both - hi.astype(F32)
        mid = rest.astype(BF16)
        low = (rest - mid.astype(F32)).astype(BF16)
        out = (
            jnp.dot(hi, regroup, preferred_element_type=F32)
            + jnp.dot(mid, regroup, preferred_element_type=F32)
            + jnp.dot(low, regroup, preferred_element_type=F32)
        )
        az[0, pair] = out[:, :TC]
        az[1, pair] = out[:, TC:]
    put(az.at[1 - z], ax.at[c, z], AZ, z_peer)
    ax[c, z] = az[z]

    for k in range(1, W):
        dg[c, k - 1] = d_ref[k]

    parts = ((z, 0), (z, 1), (1 - z, 0), (1 - z, 1))

    def send_a(part):
        piece = ax.at[(c, *parts[part])]
        over_cols(piece, piece, A + part)

    def take_a(part):
        half, pair = parts[part]
        take(A + part, ax.at[pl.ds(0, COLS - 1), half, pair])
        for q in range(COLS):
            hi, lo = split(ax[q, half, pair])
            lanes = slice((2 * q + pair) * TC, (2 * q + pair + 1) * TC)
            ah[half, :, lanes] = hi
            al[half, :, lanes] = lo

    def take_d():
        take(D, dg.at[pl.ds(0, COLS - 1)])
        for q in range(COLS):
            for k in range(3):
                hi, lo = split(dg[q, k])
                dh[k, :, q * TC:(q + 1) * TC] = hi
                dl[k, :, q * TC:(q + 1) * TC] = lo

    def minus_product(acc, i, j):
        s = WINDOW_BLOCKS.index((i, j))
        part = dot3(
            zh[i][...], zl[i][...], th[s].reshape(FULL, TC), tl[s].reshape(FULL, TC)
        ).reshape(NB - 1 - i, TR, TC)
        for k in range(i + 1, NB):
            acc[k - j - 1] -= part[k - i - 1]

    send_a(0)
    send_a(1)

    weight_copy.wait()
    weight = w_ref[0]

    pairs = []

    def to_sibling(slot, src, dst):
        copy = pltpu.make_async_remote_copy(
            src_ref=src, dst_ref=dst, send_sem=send1.at[slot], recv_sem=recv1.at[slot],
            device_id=sibling, device_id_type=MESH,
        )
        copy.start()
        pairs.append(copy)
        return copy

    above = {}

    def half_column(j):
        take(R + j, zr.at[j, pl.ds(0, 3)])
        for q in range(4):
            for m in range(4):
                hi, lo = split(zr[j, q, m].reshape(GROUPS, SUB, TC))
                bh[:, m, q] = hi
                bl[:, m, q] = lo
        part = weight * dot3(
            ah[...].reshape(8 * TR, 2 * FULL), al[...].reshape(8 * TR, 2 * FULL), bh[...].reshape(2 * FULL, TC), bl[...].reshape(2 * FULL, TC)
        )
        qs[j, 0] = part[:4 * TR]
        qs[j, 1] = part[4 * TR:]
        put(qs.at[j, 1 - z], qr.at[j], Q + j, z_peer)

    def column(j):
        blocks = NB - 1 - j
        first = blocks - 4
        take(Q + j, qr.at[j])
        q_above = qs[j, z] + qr[j]
        hi, lo = split(q_above)
        qh[first * TR:blocks * TR, :] = hi
        ql[first * TR:blocks * TR, :] = lo
        q_above = q_above.reshape(4, TR, TC)
        for m in range(4):
            pa[j, m] = q_above[m]
        above[j] = [
            to_sibling(4 * j + t, pa.at[j, 2 * t + other], ra.at[j, t]) for t in range(2)
        ]
        inside = []
        for m in range(first):
            k = j + 1 + m
            if m == 0:
                s = WINDOW_BLOCKS.index((k, j))
                q_in = -weight * dot3(
                    dh[k - 1], dl[k - 1], th[s].reshape(FULL, TC), tl[s].reshape(FULL, TC)
                )
            else:
                s = WINDOW_LATER[j][0] + m - 1
                q_in = weight * dot3(
                    dh[k - 1], dl[k - 1], wh[s].reshape(FULL, TC), wl[s].reshape(FULL, TC)
                )
            hi, lo = split(q_in)
            qh[m * TR:(m + 1) * TR, :] = hi
            ql[m * TR:(m + 1) * TR, :] = lo
            inside.append(q_in)
        for l in range(j, W):
            start = (l - j) * TR
            part = dot3(
                qh[start:blocks * TR, :], ql[start:blocks * TR, :],
                zh[l][...], zl[l][...],
                (((0,), (0,)), ((), ())),
            ).T.reshape(GROUPS, ROWS, SUB, TC)
            for q in range(ROWS):
                pw[j, l, q] = part[:, q].reshape(TR, TC)
            pw[j, l, r] += weight * d_ref[j] if l == j else inside[l - j - 1]

    def finish(j):
        slots = [1, 0] if j < 2 else [1]
        used = {t: None if 2 * t >= j else core == 1 for t in slots}
        unused = {t: None if 2 * t >= j else core == 0 for t in slots}
        copies = {}
        for t in slots:
            copies[t] = pltpu.make_async_remote_copy(
                src_ref=pw.at[j, 2 * t + other], dst_ref=rw.at[j, t],
                send_sem=send1.at[4 * j + 2 + t], recv_sem=recv1.at[4 * j + 2 + t],
                device_id=sibling, device_id_type=MESH,
            )
            when(unused[t], copies[t].start)
            later_waits.append((unused[t], copies[t].wait_send))
        yield
        for t in slots:
            def add(t=t):
                copies[t].wait_recv()
                rw[j, t] += pw[j, 2 * t + core]
                gw[j, t, r] = rw[j, t, r]
                for p in row_peers:
                    put(rw.at[j, t, p], gw.at[j, t, r], F2 + 2 * j + t, {"row": p})

            when(used[t], add)
        for t, copy in enumerate(above[j]):
            copy.wait_recv()
            hb[2 + t, j] = pa[j, 2 * t + core] + ra[j, t]
        send_out(j, 2)
        send_out(j, 3)
        yield
        for t in slots:
            def total(t=t):
                piece = gw.at[j, t, pl.ds(0, ROWS - 1)]
                pltpu.make_async_copy(piece, piece, recv.at[F2 + 2 * j + t]).wait()
                hb[t, j] = jnp.sum(gw[j, t], axis=0)

            def sent(t=t):
                piece = gw.at[j, t, pl.ds(0, ROWS - 1)]
                pltpu.make_async_copy(piece, piece, send.at[F2 + 2 * j + t]).wait()

            when(used[t], total)
            later_waits.append((used[t], sent))
            send_out(j, t)
        kb[z_hi, j] = hb[z_hi, j]
        yield
        l = 2 * z_hi + core

        @pl.when(l >= j)
        def _():
            piece = kb.at[pl.ds(0, 3), j]
            pltpu.make_async_copy(piece, piece, recv.at[F3 + j]).wait()
            chosen = (pat_ref[j, g] + (g == j).astype(jnp.int32)).astype(F32)
            out_ref[:, j, :] = jnp.sum(kb[:, j], axis=0) * chosen

        if j > 0:
            @pl.when(l < j)
            def _():
                out_ref[:, j, :] = jnp.zeros((TR, TC), F32)
        yield

    def send_out(j, t):
        condition = z_hi != t
        if 2 * t < j:
            condition = jnp.logical_and(condition, core == 1)

        def copy():
            return pltpu.make_async_remote_copy(
                src_ref=hb.at[t, j], dst_ref=kb.at[z_hi, j], send_sem=send.at[F3 + j],
                recv_sem=recv.at[F3 + j], device_id={"cfg": 2 * t + core}, device_id_type=MESH,
            )

        when(condition, lambda: copy().start())
        later_waits.append((condition, lambda: copy().wait_send()))

    hb[0:2] = jnp.zeros((2, 4, TR, TC), F32)
    for j in (2, 1, 0):
        take_t(2 - j)
        acc = [-panel(k, j) for k in range(j + 1, NB)]
        for i in range(W - 1, j + 1, -1):
            minus_product(acc, i, j)
        if j == 1:
            take_a(0)
            take_a(1)
        if j == 0:
            take_a(2)
            take_a(3)
            half_column(3)
            half_column(2)
        take_x(j + 1)
        minus_product(acc, j + 1, j)
        for m in range(NB - 1 - j):
            zx[j][c, m] = acc[m]
        if j > 0:
            send_x(j)
        send_y(j)
        if j < 2:
            send_w(j)
        if j == 2:
            send_y(3)
            take(AZ, ax.at[c, 1 - z])
            send_a(2)
            send_a(3)
        if j == 1:
            over_cols(dg.at[c], dg.at[c], D)
        if j == 0:
            send_x(0)

    steps = {}
    column(3)
    steps[3] = finish(3)
    next(steps[3])
    take_d()
    column(2)
    steps[2] = finish(2)
    next(steps[2])
    next(steps[3])
    half_column(1)
    next(steps[2])
    half_column(0)
    take_w(1)
    column(1)
    steps[1] = finish(1)
    next(steps[1])
    next(steps[1])
    take_w(0)
    take_x(0)
    column(0)
    steps[0] = finish(0)
    next(steps[0])
    next(steps[0])
    next(steps[3])
    next(steps[2])
    next(steps[1])
    next(steps[0])
    next(steps[3])
    next(steps[2])
    next(steps[1])
    next(steps[0])

    for phase, ref in waits:
        pltpu.make_async_copy(ref, ref, send.at[phase]).wait()
    for copy in pairs:
        copy.wait_send()
    for condition, action in later_waits:
        when(condition, action)


def local(sigma_above, panels, diag_inverse, pattern, cfg_weight):
    vmem = pl.BlockSpec(memory_space=pltpu.VMEM)
    smem = pl.BlockSpec(memory_space=pltpu.SMEM)
    tiles = [NB - 1 - j for j in range(W)]
    scratch = [pltpu.VMEM((ROWS, 6, TR, TC), F32)]
    scratch += [pltpu.VMEM((COLS, n, TR, TC), F32) for n in tiles]
    scratch += [pltpu.VMEM((W, 4, 4, TR, TC), F32), pltpu.VMEM((ROWS, 3, TR, TC), F32)]
    scratch += [pltpu.VMEM((2, 2, 4 * TR, TC), F32), pltpu.VMEM((COLS, 2, 2, 4 * TR, TC), F32)]
    scratch += [pltpu.VMEM((COLS, 3, TR, TC), F32)]
    scratch += [pltpu.VMEM((W, 2, 4 * TR, TC), F32), pltpu.VMEM((W, 4 * TR, TC), F32)]
    scratch += [pltpu.VMEM((2, 4 * TR, 2 * FULL), BF16)] * 2
    scratch += [pltpu.VMEM((3, TR, FULL), BF16)] * 2
    scratch += [pltpu.VMEM((6, GROUPS, ROWS, SUB, TC), BF16)] * 2
    scratch += [pltpu.VMEM((n * TR, FULL), BF16) for n in tiles] * 2
    scratch += [pltpu.VMEM((GROUPS, 4, 4, SUB, TC), BF16)] * 2
    scratch += [pltpu.VMEM((3, GROUPS, ROWS, SUB, TC), BF16)] * 2
    scratch += [pltpu.VMEM((7 * TR, TC), BF16)] * 2
    scratch += [
        pltpu.VMEM((4, 4, ROWS, TR, TC), F32),
        pltpu.VMEM((4, 4, TR, TC), F32),
        pltpu.VMEM((4, 2, ROWS, TR, TC), F32),
        pltpu.VMEM((4, 2, TR, TC), F32),
        pltpu.VMEM((4, 2, ROWS, TR, TC), F32),
        pltpu.VMEM((4, 4, TR, TC), F32),
        pltpu.VMEM((4, 4, TR, TC), F32),
        pltpu.SemaphoreType.DMA((35,)),
        pltpu.SemaphoreType.DMA((35,)),
        pltpu.SemaphoreType.DMA((16,)),
        pltpu.SemaphoreType.DMA((16,)),
        pltpu.SMEM((1,), F32),
        pltpu.SemaphoreType.DMA,
    ]
    out = pl.pallas_call(
        kernel,
        name="selected_inverse",
        out_shape=jax.ShapeDtypeStruct((TR, W, TC), F32),
        in_specs=[vmem, vmem, vmem, smem, pl.BlockSpec(memory_space=pl.ANY)],
        out_specs=vmem,
        scratch_shapes=scratch,
        compiler_params=pltpu.CompilerParams(
            collective_id=0, has_side_effects=True, vmem_limit_bytes=56 << 20
        ),
    )(
        sigma_above.reshape(4 * TR, 4, TC),
        panels.reshape(W, NB, TR, TC),
        diag_inverse.reshape(W, TR, TC),
        pattern.T,
        cfg_weight,
    )
    return out.reshape(1, GROUPS, 1, SUB, W, TC)


def solution(mesh):
    return jax.shard_map(
        local,
        mesh=mesh,
        in_specs=(
            P("cfg", None, None, "row", None, None, "col"),
            P("cfg", None, None, None, "row", None, "col"),
            P("cfg", None, None, "row", None, "col"),
            P(),
            P("cfg"),
        ),
        out_specs=P("cfg", None, "row", None, None, "col"),
        check_vma=False,
    )
```

```python
import jax
import jax.numpy as jnp
from jax import lax
from jax.experimental import pallas as pl
from jax.experimental.pallas import tpu as pltpu
from jax.sharding import PartitionSpec as P

MESH = pl.DeviceIdType.MESH
F32 = jnp.float32
BF16 = jnp.bfloat16
W = 4
NB = 8
ROWS = 8
COLS = 4
GROUPS = 4
SUB = 16
TR = 64
TC = 128
FULL = 512
WINDOW_BLOCKS = ((3, 2), (3, 1), (2, 1), (3, 0), (2, 0), (1, 0))
WINDOW_PHASES = ((0, 1), (1, 2), (3, 3))
WINDOW_LATER = {1: (0, 1), 0: (1, 2)}


def split(x):
    hi = x.astype(BF16)
    return hi, (x - hi.astype(F32)).astype(BF16)


def dot3(ah, al, bh, bl, dims=(((1,), (0,)), ((), ()))):
    def one(a, b):
        return lax.dot_general(a, b, dims, preferred_element_type=F32)

    return one(ah, bh) + (one(ah, bl) + one(al, bh))


def kernel(
    a_hbm, u_hbm, d_hbm, pat_ref, w_hbm, out_ref,
    tr, zx0, zx1, zx2, zx3, zr, zw, az, ax, dg, qs, qr,
    ah, al, dh, dl, th, tl, zh0, zh1, zh2, zh3, zl0, zl1, zl2, zl3, bh, bl, wh, wl, qh, ql,
    pw, pa, rw, ra, gw, hb, kb,
    send, recv, send1, recv1, w_ref, w_sem, a_ref, u_ref, d_ref, in_sem,
):
    zx = (zx0, zx1, zx2, zx3)
    zh, zl = (zh0, zh1, zh2, zh3), (zl0, zl1, zl2, zl3)
    g, r, c = lax.axis_index("cfg"), lax.axis_index("row"), lax.axis_index("col")
    z_hi, core = lax.div(g, 2), lax.rem(g, 2)
    y, z = lax.div(r, 2), lax.rem(r, 2)
    other = 1 - core
    row_peers = [lax.rem(r + d, ROWS) for d in range(1, ROWS)]
    y_peers = [2 * lax.rem(y + d, 4) + z for d in range(1, 4)]
    z_peer = {"row": 2 * y + 1 - z}
    col_peers = [lax.rem(c + d, COLS) for d in range(1, COLS)]
    z_peers = [lax.rem(z_hi + d, 4) for d in range(1, 4)]
    sibling = {"cfg": 2 * z_hi + other}

    weight_copy = pltpu.make_async_copy(w_hbm, w_ref, w_sem)
    weight_copy.start()
    u_copy = pltpu.make_async_copy(u_hbm, u_ref, in_sem.at[0])
    a_copy = pltpu.make_async_copy(a_hbm, a_ref, in_sem.at[1])
    d_copy = pltpu.make_async_copy(d_hbm, d_ref, in_sem.at[2])
    u_copy.start()
    a_copy.start()
    d_copy.start()
    barrier = pltpu.get_barrier_semaphore()
    everyone = [{"row": p} for p in row_peers] + [{"col": p} for p in col_peers]
    everyone += [{"cfg": 2 * p + core} for p in z_peers] + [sibling]
    for peer in everyone:
        pl.semaphore_signal(barrier, inc=1, device_id=peer, device_id_type=MESH)
    pl.semaphore_wait(barrier, len(everyone))

    waits = []
    later_waits = []

    def when(condition, action):
        if condition is None:
            action()
        else:
            pl.when(condition)(action)

    def put(src, dst, phase, peer):
        pltpu.make_async_remote_copy(
            src_ref=src, dst_ref=dst, send_sem=send.at[phase], recv_sem=recv.at[phase],
            device_id=peer, device_id_type=MESH,
        ).start()

    def take(phase, ref):
        pltpu.make_async_copy(ref, ref, recv.at[phase]).wait()
        waits.append((phase, ref))

    def over_rows(src, dst, phase):
        for p in row_peers:
            put(src, dst, phase, {"row": p})

    def over_cols(src, dst, phase):
        for p in col_peers:
            put(src, dst, phase, {"col": p})

    X, R, T, D, F2, F3, WZ, Q, AZ, A = 0, 4, 8, 11, 12, 20, 24, 26, 30, 31

    def panel(k, j):
        return u_ref[j, k] * pat_ref[j, k].astype(F32)

    def send_x(j):
        over_cols(zx[j].at[c], zx[j].at[c], X + j)

    def send_y(j):
        for m in range(4):
            zr[j, y, m] = zx[j][c, NB - 5 - j + m]
        for p in y_peers:
            put(zr.at[j, y], zr.at[j, y], R + j, {"row": p})

    def send_w(j):
        slot, count = WINDOW_LATER[j]
        for m in range(count):
            zw[r, slot + m] = zx[j][c, 1 + m]
        piece = zw.at[r, pl.ds(slot, count)]
        over_rows(piece, piece, WZ + j)

    def take_w(j):
        slot, count = WINDOW_LATER[j]
        take(WZ + j, zw.at[pl.ds(0, ROWS - 1), pl.ds(slot, count)])
        for m in range(slot, slot + count):
            for q in range(ROWS):
                hi, lo = split(zw[q, m].reshape(GROUPS, SUB, TC))
                wh[m, :, q] = hi
                wl[m, :, q] = lo

    def take_x(j):
        take(X + j, zx[j].at[pl.ds(0, COLS - 1)])
        for q in range(COLS):
            hi, lo = split(zx[j][q].reshape(-1, TC))
            zh[j][:, q * TC:(q + 1) * TC] = hi
            zl[j][:, q * TC:(q + 1) * TC] = lo

    def take_t(phase):
        first, count = WINDOW_PHASES[phase]
        take(T + phase, tr.at[pl.ds(0, ROWS - 1), pl.ds(first, count)])
        for s in range(first, first + count):
            for q in range(ROWS):
                hi, lo = split(tr[q, s].reshape(GROUPS, SUB, TC))
                th[s, :, q] = hi
                tl[s, :, q] = lo

    def send_t(phase):
        first, count = WINDOW_PHASES[phase]
        for s in range(first, first + count):
            tr[r, s] = panel(*WINDOW_BLOCKS[s])
        piece = tr.at[r, pl.ds(first, count)]
        over_rows(piece, piece, T + phase)

    u_copy.wait()
    send_t(0)
    for m in range(4):
        zx[3][c, m] = -panel(W + m, 3)
    send_x(3)
    send_t(1)

    a_copy.wait()
    d_copy.wait()
    source = lax.broadcasted_iota(jnp.int32, (2 * TC, 2 * TC), 0)
    target = lax.broadcasted_iota(jnp.int32, (2 * TC, 2 * TC), 1)
    parity = lax.rem(lax.div(source, SUB), 2)
    place = parity * TC + lax.div(source, 2 * SUB) * SUB + lax.rem(source, SUB)
    regroup = (place == target).astype(F32).astype(BF16)
    for pair in range(2):
        both = jnp.concatenate([a_ref[:, 2 * pair, :], a_ref[:, 2 * pair + 1, :]], axis=1)
        hi = both.astype(BF16)
        rest = both - hi.astype(F32)
        mid = rest.astype(BF16)
        low = (rest - mid.astype(F32)).astype(BF16)
        out = (
            jnp.dot(hi, regroup, preferred_element_type=F32)
            + jnp.dot(mid, regroup, preferred_element_type=F32)
            + jnp.dot(low, regroup, preferred_element_type=F32)
        )
        az[0, pair] = out[:, :TC]
        az[1, pair] = out[:, TC:]
    put(az.at[1 - z], ax.at[c, z], AZ, z_peer)
    ax[c, z] = az[z]

    for k in range(1, W):
        dg[c, k - 1] = d_ref[k]

    parts = ((z, 0), (z, 1), (1 - z, 0), (1 - z, 1))

    def send_a(part):
        piece = ax.at[(c, *parts[part])]
        over_cols(piece, piece, A + part)

    def take_a(part):
        half, pair = parts[part]
        take(A + part, ax.at[pl.ds(0, COLS - 1), half, pair])
        for q in range(COLS):
            hi, lo = split(ax[q, half, pair])
            lanes = slice((2 * q + pair) * TC, (2 * q + pair + 1) * TC)
            ah[half, :, lanes] = hi
            al[half, :, lanes] = lo

    def take_d():
        take(D, dg.at[pl.ds(0, COLS - 1)])
        for q in range(COLS):
            for k in range(3):
                hi, lo = split(dg[q, k])
                dh[k, :, q * TC:(q + 1) * TC] = hi
                dl[k, :, q * TC:(q + 1) * TC] = lo

    def minus_product(acc, i, j):
        s = WINDOW_BLOCKS.index((i, j))
        part = dot3(
            zh[i][...], zl[i][...], th[s].reshape(FULL, TC), tl[s].reshape(FULL, TC)
        ).reshape(NB - 1 - i, TR, TC)
        for k in range(i + 1, NB):
            acc[k - j - 1] -= part[k - i - 1]

    send_a(0)
    send_a(1)

    weight_copy.wait()
    weight = w_ref[0]

    pairs = []

    def to_sibling(slot, src, dst):
        copy = pltpu.make_async_remote_copy(
            src_ref=src, dst_ref=dst, send_sem=send1.at[slot], recv_sem=recv1.at[slot],
            device_id=sibling, device_id_type=MESH,
        )
        copy.start()
        pairs.append(copy)
        return copy

    above = {}

    def half_column(j):
        take(R + j, zr.at[j, pl.ds(0, 3)])
        for q in range(4):
            for m in range(4):
                hi, lo = split(zr[j, q, m].reshape(GROUPS, SUB, TC))
                bh[:, m, q] = hi
                bl[:, m, q] = lo
        part = weight * dot3(
            ah[...].reshape(8 * TR, 2 * FULL), al[...].reshape(8 * TR, 2 * FULL), bh[...].reshape(2 * FULL, TC), bl[...].reshape(2 * FULL, TC)
        )
        qs[j, 0] = part[:4 * TR]
        qs[j, 1] = part[4 * TR:]
        put(qs.at[j, 1 - z], qr.at[j], Q + j, z_peer)

    def column(j):
        blocks = NB - 1 - j
        first = blocks - 4
        take(Q + j, qr.at[j])
        q_above = qs[j, z] + qr[j]
        hi, lo = split(q_above)
        qh[first * TR:blocks * TR, :] = hi
        ql[first * TR:blocks * TR, :] = lo
        q_above = q_above.reshape(4, TR, TC)
        for m in range(4):
            pa[j, m] = q_above[m]
        above[j] = [
            to_sibling(4 * j + t, pa.at[j, 2 * t + other], ra.at[j, t]) for t in range(2)
        ]
        inside = []
        for m in range(first):
            k = j + 1 + m
            if m == 0:
                s = WINDOW_BLOCKS.index((k, j))
                q_in = -weight * dot3(
                    dh[k - 1], dl[k - 1], th[s].reshape(FULL, TC), tl[s].reshape(FULL, TC)
                )
            else:
                s = WINDOW_LATER[j][0] + m - 1
                q_in = weight * dot3(
                    dh[k - 1], dl[k - 1], wh[s].reshape(FULL, TC), wl[s].reshape(FULL, TC)
                )
            hi, lo = split(q_in)
            qh[m * TR:(m + 1) * TR, :] = hi
            ql[m * TR:(m + 1) * TR, :] = lo
            inside.append(q_in)
        for l in range(j, W):
            start = (l - j) * TR
            part = dot3(
                qh[start:blocks * TR, :], ql[start:blocks * TR, :],
                zh[l][...], zl[l][...],
                (((0,), (0,)), ((), ())),
            ).T.reshape(GROUPS, ROWS, SUB, TC)
            for q in range(ROWS):
                pw[j, l, q] = part[:, q].reshape(TR, TC)
            pw[j, l, r] += weight * d_ref[j] if l == j else inside[l - j - 1]

    def finish(j):
        slots = [1, 0] if j < 2 else [1]
        used = {t: None if 2 * t >= j else core == 1 for t in slots}
        unused = {t: None if 2 * t >= j else core == 0 for t in slots}
        copies = {}
        for t in slots:
            copies[t] = pltpu.make_async_remote_copy(
                src_ref=pw.at[j, 2 * t + other], dst_ref=rw.at[j, t],
                send_sem=send1.at[4 * j + 2 + t], recv_sem=recv1.at[4 * j + 2 + t],
                device_id=sibling, device_id_type=MESH,
            )
            when(unused[t], copies[t].start)
            later_waits.append((unused[t], copies[t].wait_send))
        yield
        for t in slots:
            def add(t=t):
                copies[t].wait_recv()
                rw[j, t] += pw[j, 2 * t + core]
                gw[j, t, r] = rw[j, t, r]
                for p in row_peers:
                    put(rw.at[j, t, p], gw.at[j, t, r], F2 + 2 * j + t, {"row": p})

            when(used[t], add)
        for t, copy in enumerate(above[j]):
            copy.wait_recv()
            hb[2 + t, j] = pa[j, 2 * t + core] + ra[j, t]
        send_out(j, 2)
        send_out(j, 3)
        yield
        for t in slots:
            def total(t=t):
                piece = gw.at[j, t, pl.ds(0, ROWS - 1)]
                pltpu.make_async_copy(piece, piece, recv.at[F2 + 2 * j + t]).wait()
                hb[t, j] = jnp.sum(gw[j, t], axis=0)

            def sent(t=t):
                piece = gw.at[j, t, pl.ds(0, ROWS - 1)]
                pltpu.make_async_copy(piece, piece, send.at[F2 + 2 * j + t]).wait()

            when(used[t], total)
            later_waits.append((used[t], sent))
            send_out(j, t)
        kb[z_hi, j] = hb[z_hi, j]
        yield
        l = 2 * z_hi + core

        @pl.when(l >= j)
        def _():
            piece = kb.at[pl.ds(0, 3), j]
            pltpu.make_async_copy(piece, piece, recv.at[F3 + j]).wait()
            chosen = (pat_ref[j, g] + (g == j).astype(jnp.int32)).astype(F32)
            out_ref[:, j, :] = jnp.sum(kb[:, j], axis=0) * chosen

        if j > 0:
            @pl.when(l < j)
            def _():
                out_ref[:, j, :] = jnp.zeros((TR, TC), F32)
        yield

    def send_out(j, t):
        condition = z_hi != t
        if 2 * t < j:
            condition = jnp.logical_and(condition, core == 1)

        def copy():
            return pltpu.make_async_remote_copy(
                src_ref=hb.at[t, j], dst_ref=kb.at[z_hi, j], send_sem=send.at[F3 + j],
                recv_sem=recv.at[F3 + j], device_id={"cfg": 2 * t + core}, device_id_type=MESH,
            )

        when(condition, lambda: copy().start())
        later_waits.append((condition, lambda: copy().wait_send()))

    hb[0:2] = jnp.zeros((2, 4, TR, TC), F32)
    for j in (2, 1, 0):
        take_t(2 - j)
        acc = [-panel(k, j) for k in range(j + 1, NB)]
        for i in range(W - 1, j + 1, -1):
            minus_product(acc, i, j)
        if j == 1:
            take_a(0)
            take_a(1)
        if j == 0:
            take_a(2)
            take_a(3)
            half_column(3)
            half_column(2)
            column(3)
            steps = {3: finish(3)}
            next(steps[3])
        take_x(j + 1)
        minus_product(acc, j + 1, j)
        for m in range(NB - 1 - j):
            zx[j][c, m] = acc[m]
        if j > 0:
            send_x(j)
        send_y(j)
        if j < 2:
            send_w(j)
        if j == 2:
            send_t(2)
            send_y(3)
            take(AZ, ax.at[c, 1 - z])
            send_a(2)
            send_a(3)
        if j == 1:
            over_cols(dg.at[c], dg.at[c], D)
        if j == 0:
            send_x(0)

    take_d()
    column(2)
    steps[2] = finish(2)
    next(steps[2])
    next(steps[3])
    half_column(1)
    next(steps[2])
    half_column(0)
    take_w(1)
    column(1)
    steps[1] = finish(1)
    next(steps[1])
    next(steps[1])
    take_w(0)
    take_x(0)
    column(0)
    steps[0] = finish(0)
    next(steps[0])
    next(steps[0])
    next(steps[3])
    next(steps[2])
    next(steps[1])
    next(steps[0])
    next(steps[3])
    next(steps[2])
    next(steps[1])
    next(steps[0])

    for phase, ref in waits:
        pltpu.make_async_copy(ref, ref, send.at[phase]).wait()
    for copy in pairs:
        copy.wait_send()
    for condition, action in later_waits:
        when(condition, action)


def local(sigma_above, panels, diag_inverse, pattern, cfg_weight):
    vmem = pl.BlockSpec(memory_space=pltpu.VMEM)
    smem = pl.BlockSpec(memory_space=pltpu.SMEM)
    hbm = pl.BlockSpec(memory_space=pl.ANY)
    tiles = [NB - 1 - j for j in range(W)]
    scratch = [pltpu.VMEM((ROWS, 6, TR, TC), F32)]
    scratch += [pltpu.VMEM((COLS, n, TR, TC), F32) for n in tiles]
    scratch += [pltpu.VMEM((W, 4, 4, TR, TC), F32), pltpu.VMEM((ROWS, 3, TR, TC), F32)]
    scratch += [pltpu.VMEM((2, 2, 4 * TR, TC), F32), pltpu.VMEM((COLS, 2, 2, 4 * TR, TC), F32)]
    scratch += [pltpu.VMEM((COLS, 3, TR, TC), F32)]
    scratch += [pltpu.VMEM((W, 2, 4 * TR, TC), F32), pltpu.VMEM((W, 4 * TR, TC), F32)]
    scratch += [pltpu.VMEM((2, 4 * TR, 2 * FULL), BF16)] * 2
    scratch += [pltpu.VMEM((3, TR, FULL), BF16)] * 2
    scratch += [pltpu.VMEM((6, GROUPS, ROWS, SUB, TC), BF16)] * 2
    scratch += [pltpu.VMEM((n * TR, FULL), BF16) for n in tiles] * 2
    scratch += [pltpu.VMEM((GROUPS, 4, 4, SUB, TC), BF16)] * 2
    scratch += [pltpu.VMEM((3, GROUPS, ROWS, SUB, TC), BF16)] * 2
    scratch += [pltpu.VMEM((7 * TR, TC), BF16)] * 2
    scratch += [
        pltpu.VMEM((4, 4, ROWS, TR, TC), F32),
        pltpu.VMEM((4, 4, TR, TC), F32),
        pltpu.VMEM((4, 2, ROWS, TR, TC), F32),
        pltpu.VMEM((4, 2, TR, TC), F32),
        pltpu.VMEM((4, 2, ROWS, TR, TC), F32),
        pltpu.VMEM((4, 4, TR, TC), F32),
        pltpu.VMEM((4, 4, TR, TC), F32),
        pltpu.SemaphoreType.DMA((35,)),
        pltpu.SemaphoreType.DMA((35,)),
        pltpu.SemaphoreType.DMA((16,)),
        pltpu.SemaphoreType.DMA((16,)),
        pltpu.SMEM((1,), F32),
        pltpu.SemaphoreType.DMA,
        pltpu.VMEM((4 * TR, 4, TC), F32),
        pltpu.VMEM((W, NB, TR, TC), F32),
        pltpu.VMEM((W, TR, TC), F32),
        pltpu.SemaphoreType.DMA((3,)),
    ]
    out = pl.pallas_call(
        kernel,
        name="selected_inverse",
        out_shape=jax.ShapeDtypeStruct((TR, W, TC), F32),
        in_specs=[hbm, hbm, hbm, smem, hbm],
        out_specs=vmem,
        scratch_shapes=scratch,
        compiler_params=pltpu.CompilerParams(
            collective_id=0, has_side_effects=True, vmem_limit_bytes=56 << 20
        ),
    )(
        sigma_above.reshape(4 * TR, 4, TC),
        panels.reshape(W, NB, TR, TC),
        diag_inverse.reshape(W, TR, TC),
        pattern.T,
        cfg_weight,
    )
    return out.reshape(1, GROUPS, 1, SUB, W, TC)


def solution(mesh):
    return jax.shard_map(
        local,
        mesh=mesh,
        in_specs=(
            P("cfg", None, None, "row", None, None, "col"),
            P("cfg", None, None, None, "row", None, "col"),
            P("cfg", None, None, "row", None, "col"),
            P(),
            P("cfg"),
        ),
        out_specs=P("cfg", None, "row", None, None, "col"),
        check_vma=False,
    )
```
